32 devices in a mesh: groups: 2 (over y), replica: 4 (over z), tensor: 2 (over x), section: 2 (over core).
Axes of the slice: x: 2, y: 2, z: 4, core: 2. Of those that a mesh axis runs over, the one named last changes fastest.
Arguments:
- queries: bfloat16 [8, 2, 64, 128, 128], P(('groups', 'replica'), 'section', 'tensor'), parts along dimension 0, may hold values from -0.52734375 to 0.52734375
- key_rows: bfloat16 [8, 2, 64, 128, 128], P(('groups', 'replica'), 'section', 'tensor'), parts along dimension 0, may hold values from -6 to 6
- value_rows: bfloat16 [8, 2, 64, 128, 128], P(('groups', 'replica'), 'section', 'tensor'), parts along dimension 0, may hold values from -6 to 6
- state_in: float32 [8, 2, 64, 128, 128], P(('groups', 'replica'), 'section', 'tensor'), parts along dimension 0, may hold values from -12 to 12
- lengths: int32 [8], P('groups'), parts along dimension 0, may hold values from 1 to 128, as said below
- assignment: int32 [8, 2, 64], P('groups'), parts along dimension 0, may hold values from 0 to 3, as said below
- head_rate: int32 [2, 64], P('section', 'tensor'), may hold values from 0 to 63
- decay_table: float32 [64], replicated, may hold values from 0.001953125 to 0.0390625
Outputs:
- helper_out: bfloat16 [8, 2, 64, 128, 128], P(('groups', 'replica'), 'section', 'tensor'), parts along dimension 0
- state_out: float32 [8, 2, 64, 128, 128], P(('groups', 'replica'), 'section', 'tensor'), parts along dimension 0
The draws below stay inside these ranges and needn't reach their ends.
There are 2 independent parts, one for each index of `groups`. The reference program is written for one: setup_inputs(seed, part) draws one part's arguments, and reference() takes and returns one part's arrays. A program takes and returns all parts, laid end to end along the dimension named above; an argument that names none is the same for every part. Nothing has to cross between parts.
Inputs may be any that keep to these rules, and one draw needn't show every extreme that they name: `assignment`: for each layer and tensor block of 32 heads: one replica's block names each replica at most 8 times, some pair reaches 8, and every replica is named exactly 32 times over all replicas. `lengths`: some replica's block is full.
All inputs are finite; a program needn't handle non-finite values.
Results may differ from the reference program's by a relative error of at most 0.0048.
Values may be sent and summed in bfloat16 or wider, within the bound.
A program may use at most 64 MiB of HBM per device.

```python
import math
import jax
import jax.numpy as jnp
from jax import lax

HEADS = 64
HD = 128
LC = 128
RATES = 64
LAYERS = 2
HEADS_DEV = 32
N_REPLICA = 4
N_TENSOR = 2


def draw_lengths(key, part):
    key = jax.random.fold_in(key, 7)
    first, second = jax.random.split(key)
    counts = jax.random.randint(first, (N_REPLICA,), 1, LC + 1)
    chosen = jax.random.randint(second, (), 0, N_REPLICA)
    counts = jnp.where(jnp.arange(N_REPLICA) == chosen, LC, counts)
    return counts.astype(jnp.int32)


def draw_assignment(key, part):
    key = jax.random.fold_in(key, 11)
    widest = max(N_REPLICA, HEADS_DEV)

    def one_block(block_key):
        first, second = jax.random.split(block_key)
        offsets = jax.random.permutation(first, widest)[:HEADS_DEV] % N_REPLICA
        shuffle = jax.random.permutation(second, N_REPLICA)
        sources = jnp.arange(N_REPLICA)
        return shuffle[(sources[:, None] + offsets[None, :]) % N_REPLICA]
    block_keys = jax.random.split(key, LAYERS * N_TENSOR)
    blocks = jax.vmap(one_block)(block_keys)
    blocks = blocks.reshape(LAYERS, N_TENSOR, N_REPLICA, HEADS_DEV)
    blocks = jnp.transpose(blocks, (2, 0, 1, 3)).reshape(N_REPLICA, LAYERS, HEADS)
    return blocks.astype(jnp.int32)


def set_ends(entries, rng, low, top_value):
    dims = entries.shape
    place = [jax.random.randint(jax.random.fold_in(rng, axis), (), 0, dims[axis]) for axis in range(len(dims))]
    entries = entries.at[tuple(place)].set(low)
    longest = dims.index(max(dims))
    place[longest] = (place[longest] + 1) % dims[longest]
    return entries.at[tuple(place)].set(top_value)


def steps_of(stream_key, extent, cuts, low, largest):
    level = 1.0
    for position, parts in cuts:
        steps = jax.random.uniform(jax.random.fold_in(jax.random.fold_in(stream_key, 6), position), (parts,), jnp.float32, low / len(cuts), largest / len(cuts))
        level = level * jnp.repeat(jnp.exp(steps), extent[position] // parts).reshape((-1,) + (1,) * (len(extent) - 1 - position))
    return level


def gaussian(own_key, shape, width, bound, cuts=(), dtype=jnp.bfloat16):
    drawn = jax.random.normal(own_key, shape, jnp.float32) * width
    if len(cuts) > 0:
        drawn = steps_of(own_key, shape, cuts, -0.22, 0.18) * drawn
    return jnp.clip(drawn, min=-bound, max=bound).astype(dtype)


def setup_inputs(seed: int = 0, part: int = 0) -> dict:
    arg_keys = jax.random.split(jax.random.key(seed), 9)
    own_keys = jax.random.split(jax.random.fold_in(arg_keys[8], part), 9)
    queries = gaussian(own_keys[0], (N_REPLICA, LAYERS, HEADS, LC, HD), (HD ** -0.5), 0.52734375, ((0, 4), (1, 2), (2, 2)))
    key_rows = gaussian(own_keys[1], (N_REPLICA, LAYERS, HEADS, LC, HD), 1.0, 6.0, ((0, 4), (1, 2), (2, 2)))
    value_rows = gaussian(own_keys[2], (N_REPLICA, LAYERS, HEADS, LC, HD), 1.0, 6.0, ((0, 4), (1, 2), (2, 2)))
    state_in = gaussian(own_keys[3], (N_REPLICA, LAYERS, HEADS, HD, HD), 2.0, 12.0, ((0, 4), (1, 2), (2, 2)), jnp.float32)
    lengths = draw_lengths(jax.random.fold_in(jax.random.fold_in(arg_keys[8], part), 71), part)
    assignment = draw_assignment(jax.random.fold_in(jax.random.fold_in(arg_keys[8], part), 71), part)
    head_rate = set_ends(jax.random.randint(arg_keys[6], (LAYERS, HEADS), 0, RATES), jax.random.fold_in(arg_keys[6], 1), 0, RATES - 1).astype(jnp.int32)
    decay_table = jnp.clip(jnp.exp(jax.random.uniform(arg_keys[7], (RATES,), jnp.float32, math.log(0.001953125), math.log(0.0390625))), 0.001953125, 0.0390625)
    return {"queries": queries, "key_rows": key_rows, "value_rows": value_rows, "state_in": state_in, "lengths": lengths, "assignment": assignment, "head_rate": head_rate, "decay_table": decay_table}


def inter_part(query_rows, state, rate):
    steps = jnp.arange(query_rows.shape[1]).astype(jnp.float32) + 1.0
    powers = jnp.exp(-rate[:, None] * steps[None, :])
    mixed = jnp.einsum("bld,bde->ble", query_rows.astype(jnp.float32), state, precision=lax.Precision.HIGHEST)
    return powers[:, :, None] * mixed


def intra_part(query_rows, key_block, value_block, rate):
    positions = jnp.arange(query_rows.shape[1])
    gaps = (positions[:, None] - positions[None, :]).astype(jnp.float32)
    causal = positions[:, None] >= positions[None, :]
    scores = jnp.einsum("bid,bjd->bij", query_rows.astype(jnp.float32), key_block.astype(jnp.float32))
    weight = jnp.where(causal[None], jnp.exp(-rate[:, None, None] * jnp.maximum(gaps, 0.0)[None]), 0.0)
    probs = (scores * weight).astype(jnp.bfloat16)
    return jnp.einsum("bij,bjd->bid", probs.astype(jnp.float32), value_block.astype(jnp.float32))


def delta_part(key_block, value_block, rate, counts):
    positions = jnp.arange(key_block.shape[1])
    filled = positions[None, :] < counts[:, None]
    remain = (counts[:, None] - 1 - positions[None, :]).astype(jnp.float32)
    weight = jnp.where(filled, jnp.exp(-rate[:, None] * jnp.maximum(remain, 0.0)), 0.0)
    scaled = key_block.astype(jnp.float32) * weight[:, :, None]
    return jnp.einsum("bjd,bje->bde", scaled, value_block.astype(jnp.float32), precision=lax.Precision.HIGHEST)


def finish_rows(intra, inter, counts):
    positions = jnp.arange(intra.shape[1])
    filled = positions[None, :] < counts[:, None]
    return jnp.where(filled[:, :, None], intra + inter, 0.0).astype(jnp.bfloat16)


def end_state(state, delta, rate, counts):
    return jnp.exp(-rate * counts.astype(jnp.float32))[:, None, None] * state + delta


def block_ranks(targets):
    order = jnp.arange(targets.shape[-1])
    same = targets[..., :, None] == targets[..., None, :]
    earlier = order[None, :] < order[:, None]
    return jnp.sum(same & earlier, axis=-1).astype(jnp.int32)


def reference(queries, key_rows, value_rows, state_in, lengths, assignment, head_rate, decay_table):
    picks = head_rate[..., None] == jnp.arange(decay_table.shape[0])[None, None, :]
    rates = jnp.sum(jnp.where(picks, decay_table[None, None, :], 0.0), axis=-1)
    flat_rate = rates.reshape(-1)
    batch = LAYERS * HEADS

    blocks = assignment.reshape(N_REPLICA, LAYERS, N_TENSOR, HEADS_DEV)
    blocks = jnp.transpose(blocks, (1, 2, 0, 3)).reshape(LAYERS, N_TENSOR, N_REPLICA * HEADS_DEV)
    ranks = block_ranks(blocks).reshape(LAYERS, N_TENSOR, N_REPLICA, HEADS_DEV)
    ranks = jnp.transpose(ranks, (2, 0, 1, 3)).reshape(N_REPLICA, LAYERS, HEADS)
    tensor_block = (jnp.arange(HEADS).astype(jnp.int32) // HEADS_DEV)[None, None, :]
    slot_index = (tensor_block * HEADS_DEV + ranks).astype(jnp.int32)
    layer_index = jnp.broadcast_to(jnp.arange(LAYERS).astype(jnp.int32)[None, :, None], (N_REPLICA, LAYERS, HEADS))
    carried = state_in[assignment, layer_index, slot_index]

    def per_replica(items):
        query_rows, key_block, value_block, state, count = items
        query_rows = query_rows.reshape(batch, LC, HD)
        key_block = key_block.reshape(batch, LC, HD)
        value_block = value_block.reshape(batch, LC, HD)
        state = state.reshape(batch, HD, HD)
        counts = jnp.full((batch,), count, jnp.int32)
        inter = inter_part(query_rows, state, flat_rate)
        intra = intra_part(query_rows, key_block, value_block, flat_rate)
        delta = delta_part(key_block, value_block, flat_rate, counts)
        result = finish_rows(intra, inter, counts)
        final = end_state(state, delta, flat_rate, counts)
        return result.reshape(LAYERS, HEADS, LC, HD), final.reshape(LAYERS, HEADS, HD, HD)

    results, finals = lax.map(per_replica, (queries, key_rows, value_rows, carried, lengths))
    helper_out = jnp.zeros((N_REPLICA, LAYERS, HEADS, LC, HD), jnp.bfloat16)
    helper_out = helper_out.at[assignment, layer_index, slot_index].set(results)
    state_out = jnp.zeros((N_REPLICA, LAYERS, HEADS, HD, HD), jnp.float32)
    state_out = state_out.at[assignment, layer_index, slot_index].set(finals)
    return helper_out, state_out
```

```python
import functools

import jax
import jax.numpy as jnp
from jax import lax
from jax.experimental import pallas as pl
from jax.experimental.pallas import tpu as pltpu
from jax.sharding import PartitionSpec as P

MESH = pl.DeviceIdType.MESH


def item(query, key, value, state, rate, count, gaps, rows):
    size = state.shape[1]
    scores = lax.dot_general(
        query, key, (((1,), (1,)), ((), ())), preferred_element_type=jnp.float32
    )
    weight = jnp.where(gaps >= 0.0, jnp.exp(-rate * jnp.maximum(gaps, 0.0)), 0.0)
    probs = (scores * weight).astype(jnp.bfloat16)
    intra = jnp.dot(probs, value, preferred_element_type=jnp.float32)
    high = state.astype(jnp.bfloat16)
    low = (state - high.astype(jnp.float32)).astype(jnp.bfloat16)
    mixed = jnp.dot(
        query, jnp.concatenate([high, low], axis=1), preferred_element_type=jnp.float32
    )
    mixed = mixed[:, :size] + mixed[:, size:]
    powers = jnp.exp(-rate * (rows.astype(jnp.float32) + 1.0))
    result = jnp.where(rows < count, intra + powers * mixed, 0.0).astype(jnp.bfloat16)
    remain = jnp.maximum(count - 1 - rows, 0).astype(jnp.float32)
    fade = jnp.where(rows < count, jnp.exp(-rate * remain), 0.0)
    scaled = value.astype(jnp.float32) * fade
    high = scaled.astype(jnp.bfloat16)
    low = (scaled - high.astype(jnp.float32)).astype(jnp.bfloat16)
    delta = lax.dot_general(
        key,
        jnp.concatenate([high, low], axis=1),
        (((0,), (0,)), ((), ())),
        preferred_element_type=jnp.float32,
    )
    delta = delta[:, :size] + delta[:, size:]
    kept = jnp.exp(jnp.full((1, size), -rate * count.astype(jnp.float32)))
    return result, kept * state + delta


def kernel(
    replicas, per_pair, full,
    order_ref, chosen_ref, rate_ref, count_ref, q_ref, k_ref, v_ref, state_hbm,
    rows_hbm, final_hbm,
    send, recv, state_ref, rows_ref, final_ref,
    state_sem, send_sem, recv_sem, rows_sem, final_sem,
):
    heads, tokens = q_ref.shape[0], q_ref.shape[1]
    me = lax.axis_index("replica")

    barrier = pltpu.get_barrier_semaphore()
    for step in range(1, replicas):
        pl.semaphore_signal(
            barrier, inc=1, device_id={"replica": lax.rem(me + step, replicas)},
            device_id_type=MESH,
        )
    state_copy = pltpu.make_async_copy(state_hbm, state_ref, state_sem)
    state_copy.start()

    def stage(target, buffer, place):
        head = order_ref[target]
        buffer[place, 0] = q_ref[head]
        buffer[place, 1] = k_ref[head]
        buffer[place, 2] = v_ref[head]

    def outgoing(step, rank):
        return pltpu.make_async_remote_copy(
            src_ref=send.at[step * per_pair + rank],
            dst_ref=recv.at[me * per_pair + rank],
            send_sem=send_sem.at[step * per_pair + rank],
            recv_sem=recv_sem.at[me * per_pair + rank],
            device_id={"replica": lax.rem(me + step, replicas)},
            device_id_type=MESH,
        )

    for rank in range(per_pair):
        for step in range(1, replicas):
            target = lax.rem(me + step, replicas)
            stage(target * per_pair + rank, send, step * per_pair + rank)
            if rank == 0 and step == 1:
                pl.semaphore_wait(barrier, replicas - 1)
            outgoing(step, rank).start()

    def stage_own(rank, carry):
        stage(me * per_pair + rank, recv, me * per_pair + rank)
        return carry

    lax.fori_loop(0, per_pair, stage_own, 0)

    across = lax.broadcasted_iota(jnp.int32, (tokens, tokens), 1)
    down = lax.broadcasted_iota(jnp.int32, (tokens, tokens), 0)
    gaps = (down - across).astype(jnp.float32)
    rows = lax.broadcasted_iota(jnp.int32, (tokens, q_ref.shape[2]), 0)

    def out_copies(slot):
        return (
            pltpu.make_async_copy(rows_ref.at[slot], rows_hbm.at[slot], rows_sem.at[slot]),
            pltpu.make_async_copy(final_ref.at[slot], final_hbm.at[slot], final_sem.at[slot]),
        )

    def compute(slot, block):
        result, final = item(
            recv[block, 0], recv[block, 1], recv[block, 2], state_ref[slot],
            rate_ref[slot], count_ref[slot], gaps, rows,
        )
        rows_ref[slot] = result
        final_ref[slot] = final
        for copy in out_copies(slot):
            copy.start()

    def arrived(block):
        pltpu.make_async_copy(recv.at[block], recv.at[block], recv_sem.at[block]).wait()

    state_copy.wait()
    if full:

        def own(rank, carry):
            slot = me * per_pair + rank
            compute(slot, slot)
            return carry

        lax.fori_loop(0, per_pair, own, 0)

        def others(rank, carry):
            for step in range(1, replicas):
                slot = lax.rem(me + replicas - step, replicas) * per_pair + rank
                arrived(slot)
                compute(slot, slot)
            return carry

        lax.fori_loop(0, per_pair, others, 0)
    else:
        for rank in range(per_pair):
            for step in range(1, replicas):
                arrived(lax.rem(me + step, replicas) * per_pair + rank)

        def each(slot, carry):
            compute(slot, chosen_ref[slot])
            return carry

        lax.fori_loop(0, heads, each, 0)

    for rank in range(per_pair):
        for step in range(1, replicas):
            outgoing(step, rank).wait_send()

    def drain(slot, carry):
        for copy in out_copies(slot):
            copy.wait()
        return carry

    lax.fori_loop(0, heads, drain, 0)


def local(queries, key_rows, value_rows, state_in, lengths, assignment, head_rate, decay_table):
    query_rows, key_block, value_block = queries[0, 0], key_rows[0, 0], value_rows[0, 0]
    held_state = state_in[0, 0]
    heads, tokens, size = query_rows.shape
    replicas = lax.axis_size("replica")
    per_pair = max(1, heads // replicas)
    slots = replicas * per_pair
    full = slots == heads
    myself = lax.axis_index("replica")
    my_layer = lax.axis_index("section")
    my_block = lax.axis_index("tensor")
    targets = lax.dynamic_slice(
        assignment, (jnp.int32(0), my_layer, my_block * heads), (replicas, 1, heads)
    )[:, 0, :]
    number = jnp.arange(heads, dtype=jnp.int32)
    earlier = number[None, :] < number[:, None]
    own = lax.dynamic_index_in_dim(targets, myself, 0, keepdims=False)
    own_rank = jnp.sum((own[:, None] == own[None, :]) & earlier, axis=1, dtype=jnp.int32)
    place = own * per_pair + own_rank
    order = jnp.sum(
        jnp.where(place[None, :] == jnp.arange(slots)[:, None], number[None, :], 0),
        axis=1, dtype=jnp.int32,
    )
    mine = targets == myself
    rank = jnp.sum(mine[:, None, :] & earlier[None], axis=2, dtype=jnp.int32)
    hit = mine[:, None, :] & (rank[:, None, :] == jnp.arange(per_pair)[None, :, None])
    hit = hit.reshape(slots, heads)
    picks = head_rate[0][:, None] == jnp.arange(decay_table.shape[0])[None, :]
    head_decay = jnp.sum(jnp.where(picks, decay_table[None, :], 0.0), axis=1)
    rates = jnp.sum(jnp.where(hit, head_decay[None, :], 0.0), axis=1)
    counts = jnp.repeat(lengths, per_pair)
    if full:
        chosen = jnp.zeros((1,), jnp.int32)
    else:
        taken = jnp.any(hit, axis=1)
        before = jnp.cumsum(taken.astype(jnp.int32)) - 1
        spot = taken[None, :] & (before[None, :] == number[:, None])
        chosen = jnp.sum(
            jnp.where(spot, jnp.arange(slots, dtype=jnp.int32)[None, :], 0),
            axis=1, dtype=jnp.int32,
        )
        rates = jnp.sum(jnp.where(spot, rates[None, :], 0.0), axis=1)
        counts = jnp.sum(jnp.where(spot, counts[None, :], 0), axis=1, dtype=jnp.int32)
    smem = pl.BlockSpec(memory_space=pltpu.SMEM)
    vmem = pl.BlockSpec(memory_space=pltpu.VMEM)
    anywhere = pl.BlockSpec(memory_space=pl.ANY)
    rows_out, final_out = pl.pallas_call(
        functools.partial(kernel, replicas, per_pair, full),
        out_shape=(
            jax.ShapeDtypeStruct((heads, tokens, size), jnp.bfloat16),
            jax.ShapeDtypeStruct((heads, size, size), jnp.float32),
        ),
        in_specs=[smem] * 4 + [vmem] * 3 + [anywhere],
        out_specs=(anywhere, anywhere),
        scratch_shapes=[
            pltpu.VMEM((slots, 3, tokens, size), jnp.bfloat16),
            pltpu.VMEM((slots, 3, tokens, size), jnp.bfloat16),
            pltpu.VMEM((heads, size, size), jnp.float32),
            pltpu.VMEM((heads, tokens, size), jnp.bfloat16),
            pltpu.VMEM((heads, size, size), jnp.float32),
            pltpu.SemaphoreType.DMA,
            pltpu.SemaphoreType.DMA((slots,)),
            pltpu.SemaphoreType.DMA((slots,)),
            pltpu.SemaphoreType.DMA((heads,)),
            pltpu.SemaphoreType.DMA((heads,)),
        ],
        compiler_params=pltpu.CompilerParams(
            collective_id=0, has_side_effects=True, vmem_limit_bytes=24 * 1024 * 1024
        ),
    )(order, chosen, rates, counts, query_rows, key_block, value_block, held_state)
    return (rows_out[None, None], final_out[None, None])


def solution(mesh):
    in_specs = (
        P(("groups", "replica"), "section", "tensor", None, None),
        P(("groups", "replica"), "section", "tensor", None, None),
        P(("groups", "replica"), "section", "tensor", None, None),
        P(("groups", "replica"), "section", "tensor", None, None),
        P("groups"),
        P("groups", None, None),
        P("section", "tensor"),
        P(),
    )
    out_specs = (
        P(("groups", "replica"), "section", "tensor", None, None),
        P(("groups", "replica"), "section", "tensor", None, None),
    )
    return jax.shard_map(local, mesh=mesh, in_specs=in_specs, out_specs=out_specs, check_vma=False)
```

```python
import functools

import jax
import jax.numpy as jnp
from jax import lax
from jax.experimental import pallas as pl
from jax.experimental.pallas import tpu as pltpu
from jax.sharding import PartitionSpec as P

MESH = pl.DeviceIdType.MESH


def item(query, key, value, state, rate, count, gaps, rows):
    size = state.shape[1]
    scores = lax.dot_general(
        query, key, (((1,), (1,)), ((), ())), preferred_element_type=jnp.float32
    )
    weight = jnp.where(gaps >= 0.0, jnp.exp(-rate * jnp.maximum(gaps, 0.0)), 0.0)
    probs = (scores * weight).astype(jnp.bfloat16)
    intra = jnp.dot(probs, value, preferred_element_type=jnp.float32)
    high = state.astype(jnp.bfloat16)
    low = (state - high.astype(jnp.float32)).astype(jnp.bfloat16)
    mixed = jnp.dot(
        query, jnp.concatenate([high, low], axis=1), preferred_element_type=jnp.float32
    )
    mixed = mixed[:, :size] + mixed[:, size:]
    powers = jnp.exp(-rate * (rows.astype(jnp.float32) + 1.0))
    result = jnp.where(rows < count, intra + powers * mixed, 0.0).astype(jnp.bfloat16)
    remain = jnp.maximum(count - 1 - rows, 0).astype(jnp.float32)
    fade = jnp.where(rows < count, jnp.exp(-rate * remain), 0.0)
    scaled = value.astype(jnp.float32) * fade
    high = scaled.astype(jnp.bfloat16)
    low = (scaled - high.astype(jnp.float32)).astype(jnp.bfloat16)
    delta = lax.dot_general(
        key,
        jnp.concatenate([high, low], axis=1),
        (((0,), (0,)), ((), ())),
        preferred_element_type=jnp.float32,
    )
    delta = delta[:, :size] + delta[:, size:]
    kept = jnp.exp(jnp.full((1, size), -rate * count.astype(jnp.float32)))
    return result, kept * state + delta


def kernel(
    replicas, per_pair, full,
    asg_ref, length_ref, head_rate_ref, table_ref, q_hbm, k_hbm, v_hbm, state_hbm,
    rows_hbm, final_hbm,
    q_ref, k_ref, v_ref, send, recv, state_ref, rows_ref, final_ref,
    order_vmem, own_smem, order_smem,
    load_sem, order_sem, send_sem, recv_sem, rows_sem, final_sem,
):
    heads, tokens = q_ref.shape[0], q_ref.shape[1]
    me = lax.axis_index("replica")
    layer = lax.axis_index("section")
    first = lax.axis_index("tensor") * heads

    barrier = pltpu.get_barrier_semaphore()
    for step in range(1, replicas):
        pl.semaphore_signal(
            barrier, inc=1, device_id={"replica": lax.rem(me + step, replicas)},
            device_id_type=MESH,
        )
    loads = [
        pltpu.make_async_copy(source, target, load_sem.at[number])
        for number, (source, target) in enumerate(
            ((q_hbm, q_ref), (k_hbm, k_ref), (v_hbm, v_ref), (state_hbm, state_ref))
        )
    ]
    for load in loads:
        load.start()

    width = asg_ref.shape[2]
    lanes = order_vmem.shape[2]
    layers = lax.broadcasted_iota(jnp.int32, (asg_ref.shape[1], width), 0)
    col = lax.broadcasted_iota(jnp.int32, (width, width), 1)
    row = lax.broadcasted_iota(jnp.int32, (width, width), 0)
    inside = (row >= first) & (row < first + heads)
    counted = (col >= first) & (col < row)
    pair = lax.broadcasted_iota(jnp.int32, (width, lanes), 1)
    head = lax.broadcasted_iota(jnp.int32, (width, lanes), 0) - first + 1

    def find(replica):
        named = jnp.sum(
            jnp.where(layers == layer, asg_ref[replica], 0), axis=0, keepdims=True
        )
        along = jnp.broadcast_to(named, (width, width))
        down = jnp.sum(jnp.where(row == col, along, 0), axis=1, keepdims=True)
        rank = jnp.sum(
            jnp.where(counted & (down == along), 1, 0), axis=1, keepdims=True
        )
        place = jnp.where(inside[:, :1], down * per_pair + rank, -1)
        order_vmem[replica] = (
            jnp.sum(jnp.where(place == pair, head, 0), axis=0, keepdims=True) - 1
        )

    find(me)
    own_copy = pltpu.make_async_copy(order_vmem.at[me], own_smem, order_sem.at[0])
    own_copy.start()
    for load in loads[:3]:
        load.wait()
    own_copy.wait()

    def stage(target, buffer, place):
        head = own_smem[0, target]
        if not full:
            head = jnp.maximum(head, 0)
        buffer[place, 0] = q_ref[head]
        buffer[place, 1] = k_ref[head]
        buffer[place, 2] = v_ref[head]

    def outgoing(step, rank):
        return pltpu.make_async_remote_copy(
            src_ref=send.at[step * per_pair + rank],
            dst_ref=recv.at[me * per_pair + rank],
            send_sem=send_sem.at[step * per_pair + rank],
            recv_sem=recv_sem.at[me * per_pair + rank],
            device_id={"replica": lax.rem(me + step, replicas)},
            device_id_type=MESH,
        )

    for rank in range(per_pair):
        for step in range(1, replicas):
            target = lax.rem(me + step, replicas)
            stage(target * per_pair + rank, send, step * per_pair + rank)
            if rank == 0 and step == 1:
                pl.semaphore_wait(barrier, replicas - 1)
            outgoing(step, rank).start()

    def find_other(step, carry):
        find(lax.rem(me + step, replicas))
        return carry

    lax.fori_loop(1, replicas, find_other, 0)
    order_copy = pltpu.make_async_copy(order_vmem, order_smem, order_sem.at[1])
    order_copy.start()

    def stage_own(rank, carry):
        stage(me * per_pair + rank, recv, me * per_pair + rank)
        return carry

    lax.fori_loop(0, per_pair, stage_own, 0)

    across = lax.broadcasted_iota(jnp.int32, (tokens, tokens), 1)
    down = lax.broadcasted_iota(jnp.int32, (tokens, tokens), 0)
    gaps = (down - across).astype(jnp.float32)
    rows = lax.broadcasted_iota(jnp.int32, (tokens, q_ref.shape[2]), 0)

    def out_copies(slot):
        return (
            pltpu.make_async_copy(rows_ref.at[slot], rows_hbm.at[slot], rows_sem.at[slot]),
            pltpu.make_async_copy(final_ref.at[slot], final_hbm.at[slot], final_sem.at[slot]),
        )

    def compute(slot, source, rank):
        block = source * per_pair + rank
        head = jnp.maximum(order_smem[source, 0, me * per_pair + rank], 0)
        result, final = item(
            recv[block, 0], recv[block, 1], recv[block, 2], state_ref[slot],
            table_ref[head_rate_ref[0, head]], length_ref[source], gaps, rows,
        )
        rows_ref[slot] = result
        final_ref[slot] = final
        for copy in out_copies(slot):
            copy.start()

    def arrived(block):
        pltpu.make_async_copy(recv.at[block], recv.at[block], recv_sem.at[block]).wait()

    loads[3].wait()
    order_copy.wait()
    if full:

        def own(rank, carry):
            compute(me * per_pair + rank, me, rank)
            return carry

        lax.fori_loop(0, per_pair, own, 0)

        def others(rank, carry):
            for step in range(1, replicas):
                source = lax.rem(me + replicas - step, replicas)
                arrived(source * per_pair + rank)
                compute(source * per_pair + rank, source, rank)
            return carry

        lax.fori_loop(0, per_pair, others, 0)
    else:
        for rank in range(per_pair):
            for step in range(1, replicas):
                arrived(lax.rem(me + step, replicas) * per_pair + rank)

        def each(slot, carry):
            def scan(block, found):
                seen, chosen = found
                taken = order_smem[block // per_pair, 0, me * per_pair + block % per_pair] >= 0
                chosen = jnp.where(taken & (seen == slot), block, chosen)
                return seen + jnp.where(taken, 1, 0), chosen

            chosen = lax.fori_loop(
                0, replicas * per_pair, scan, (jnp.int32(0), jnp.int32(0))
            )[1]
            compute(slot, chosen // per_pair, chosen % per_pair)
            return carry

        lax.fori_loop(0, heads, each, 0)

    for rank in range(per_pair):
        for step in range(1, replicas):
            outgoing(step, rank).wait_send()

    def drain(slot, carry):
        for copy in out_copies(slot):
            copy.wait()
        return carry

    lax.fori_loop(0, heads, drain, 0)


def local(queries, key_rows, value_rows, state_in, lengths, assignment, head_rate, decay_table):
    heads, tokens, size = queries.shape[2:]
    replicas = lax.axis_size("replica")
    per_pair = max(1, heads // replicas)
    slots = replicas * per_pair
    lanes = -(-slots // 128) * 128
    smem = pl.BlockSpec(memory_space=pltpu.SMEM)
    vmem = pl.BlockSpec(memory_space=pltpu.VMEM)
    held = pl.BlockSpec(memory_space=pltpu.HBM)
    anywhere = pl.BlockSpec(memory_space=pl.ANY)
    block = pltpu.VMEM((heads, tokens, size), jnp.bfloat16)
    rows_out, final_out = pl.pallas_call(
        functools.partial(kernel, replicas, per_pair, slots == heads),
        out_shape=(
            jax.ShapeDtypeStruct((heads, tokens, size), jnp.bfloat16),
            jax.ShapeDtypeStruct((heads, size, size), jnp.float32),
        ),
        in_specs=[vmem] + [smem] * 3 + [held] * 4,
        out_specs=(anywhere, anywhere),
        scratch_shapes=[
            block, block, block,
            pltpu.VMEM((slots, 3, tokens, size), jnp.bfloat16),
            pltpu.VMEM((slots, 3, tokens, size), jnp.bfloat16),
            pltpu.VMEM((heads, size, size), jnp.float32),
            block,
            pltpu.VMEM((heads, size, size), jnp.float32),
            pltpu.VMEM((replicas, 1, lanes), jnp.int32),
            pltpu.SMEM((1, lanes), jnp.int32),
            pltpu.SMEM((replicas, 1, lanes), jnp.int32),
            pltpu.SemaphoreType.DMA((4,)),
            pltpu.SemaphoreType.DMA((2,)),
            pltpu.SemaphoreType.DMA((slots,)),
            pltpu.SemaphoreType.DMA((slots,)),
            pltpu.SemaphoreType.DMA((heads,)),
            pltpu.SemaphoreType.DMA((heads,)),
        ],
        compiler_params=pltpu.CompilerParams(
            collective_id=0, has_side_effects=True, vmem_limit_bytes=56 * 1024 * 1024
        ),
    )(
        assignment, lengths, head_rate, decay_table,
        queries[0, 0], key_rows[0, 0], value_rows[0, 0], state_in[0, 0],
    )
    return (rows_out[None, None], final_out[None, None])


def solution(mesh):
    in_specs = (
        P(("groups", "replica"), "section", "tensor", None, None),
        P(("groups", "replica"), "section", "tensor", None, None),
        P(("groups", "replica"), "section", "tensor", None, None),
        P(("groups", "replica"), "section", "tensor", None, None),
        P("groups"),
        P("groups", None, None),
        P("section", "tensor"),
        P(),
    )
    out_specs = (
        P(("groups", "replica"), "section", "tensor", None, None),
        P(("groups", "replica"), "section", "tensor", None, None),
    )
    return jax.shard_map(local, mesh=mesh, in_specs=in_specs, out_specs=out_specs, check_vma=False)
```

```python
import functools

import jax
import jax.numpy as jnp
from jax import lax
from jax.experimental import pallas as pl
from jax.experimental.pallas import tpu as pltpu
from jax.sharding import PartitionSpec as P

MESH = pl.DeviceIdType.MESH


def item(query, key, value, state, rate, count, gaps, rows):
    size = state.shape[1]
    scores = lax.dot_general(
        query, key, (((1,), (1,)), ((), ())), preferred_element_type=jnp.float32
    )
    weight = jnp.where(gaps >= 0.0, jnp.exp(-rate * jnp.maximum(gaps, 0.0)), 0.0)
    probs = (scores * weight).astype(jnp.bfloat16)
    intra = jnp.dot(probs, value, preferred_element_type=jnp.float32)
    high = state.astype(jnp.bfloat16)
    low = (state - high.astype(jnp.float32)).astype(jnp.bfloat16)
    mixed = jnp.dot(
        query, jnp.concatenate([high, low], axis=1), preferred_element_type=jnp.float32
    )
    mixed = mixed[:, :size] + mixed[:, size:]
    powers = jnp.exp(-rate * (rows.astype(jnp.float32) + 1.0))
    result = jnp.where(rows < count, intra + powers * mixed, 0.0).astype(jnp.bfloat16)
    remain = jnp.maximum(count - 1 - rows, 0).astype(jnp.float32)
    fade = jnp.where(rows < count, jnp.exp(-rate * remain), 0.0)
    scaled = value.astype(jnp.float32) * fade
    high = scaled.astype(jnp.bfloat16)
    low = (scaled - high.astype(jnp.float32)).astype(jnp.bfloat16)
    delta = lax.dot_general(
        key,
        jnp.concatenate([high, low], axis=1),
        (((0,), (0,)), ((), ())),
        preferred_element_type=jnp.float32,
    )
    delta = delta[:, :size] + delta[:, size:]
    kept = jnp.exp(jnp.full((1, size), -rate * count.astype(jnp.float32)))
    return result, kept * state + delta


def kernel(
    replicas, per_pair, full,
    asg_ref, length_ref, head_rate_ref, table_ref, q_hbm, k_hbm, v_hbm, state_hbm,
    rows_ref, final_ref,
    q_ref, k_ref, v_ref, send, recv, state_ref,
    order_vmem, own_smem, order_smem,
    load_sem, order_sem, send_sem, recv_sem,
):
    heads, tokens = q_ref.shape[0], q_ref.shape[1]
    me = lax.axis_index("replica")
    layer = lax.axis_index("section")
    first = lax.axis_index("tensor") * heads

    half = replicas // 2
    side, spot = me // half, me % half

    def receiver(step):
        if step <= half:
            return (1 - side) * half + (spot + step - 1) % half
        return side * half + (spot + step - half) % half

    def sender(step):
        if step <= half:
            return (1 - side) * half + (spot + half - (step - 1)) % half
        return side * half + (spot + half - (step - half)) % half

    barrier = pltpu.get_barrier_semaphore()
    for step in range(1, replicas):
        pl.semaphore_signal(
            barrier, inc=1, device_id={"replica": lax.rem(me + step, replicas)},
            device_id_type=MESH,
        )
    loads = [
        pltpu.make_async_copy(source, target, load_sem.at[number])
        for number, (source, target) in enumerate(
            ((q_hbm, q_ref), (k_hbm, k_ref), (v_hbm, v_ref), (state_hbm, state_ref))
        )
    ]
    for load in loads:
        load.start()

    width = asg_ref.shape[2]
    lanes = order_vmem.shape[2]
    layers = lax.broadcasted_iota(jnp.int32, (asg_ref.shape[1], width), 0)
    col = lax.broadcasted_iota(jnp.int32, (width, width), 1)
    row = lax.broadcasted_iota(jnp.int32, (width, width), 0)
    inside = (row >= first) & (row < first + heads)
    counted = (col >= first) & (col < row)
    pair = lax.broadcasted_iota(jnp.int32, (width, lanes), 1)
    head = lax.broadcasted_iota(jnp.int32, (width, lanes), 0) - first + 1

    def find(replica):
        named = jnp.sum(
            jnp.where(layers == layer, asg_ref[replica], 0), axis=0, keepdims=True
        )
        along = jnp.broadcast_to(named, (width, width))
        down = jnp.sum(jnp.where(row == col, along, 0), axis=1, keepdims=True)
        rank = jnp.sum(
            jnp.where(counted & (down == along), 1, 0), axis=1, keepdims=True
        )
        place = jnp.where(inside[:, :1], down * per_pair + rank, -1)
        order_vmem[replica] = (
            jnp.sum(jnp.where(place == pair, head, 0), axis=0, keepdims=True) - 1
        )

    find(me)
    own_copy = pltpu.make_async_copy(order_vmem.at[me], own_smem, order_sem.at[0])
    own_copy.start()
    for load in loads[:3]:
        load.wait()
    own_copy.wait()

    def stage(target, buffer, place):
        head = own_smem[0, target]
        if not full:
            head = jnp.maximum(head, 0)
        buffer[place, 0] = q_ref[head]
        buffer[place, 1] = k_ref[head]
        buffer[place, 2] = v_ref[head]

    def outgoing(step, rank):
        return pltpu.make_async_remote_copy(
            src_ref=send.at[step * per_pair + rank],
            dst_ref=recv.at[me * per_pair + rank],
            send_sem=send_sem.at[step * per_pair + rank],
            recv_sem=recv_sem.at[me * per_pair + rank],
            device_id={"replica": receiver(step)},
            device_id_type=MESH,
        )

    for rank in range(per_pair):
        for step in range(1, replicas):
            target = receiver(step)
            stage(target * per_pair + rank, send, step * per_pair + rank)
            if rank == 0 and step == 1:
                pl.semaphore_wait(barrier, replicas - 1)
            outgoing(step, rank).start()

    def find_other(step, carry):
        find(lax.rem(me + step, replicas))
        return carry

    lax.fori_loop(1, replicas, find_other, 0)
    order_copy = pltpu.make_async_copy(order_vmem, order_smem, order_sem.at[1])
    order_copy.start()

    def stage_own(rank, carry):
        stage(me * per_pair + rank, recv, me * per_pair + rank)
        return carry

    lax.fori_loop(0, per_pair, stage_own, 0)

    across = lax.broadcasted_iota(jnp.int32, (tokens, tokens), 1)
    down = lax.broadcasted_iota(jnp.int32, (tokens, tokens), 0)
    gaps = (down - across).astype(jnp.float32)
    rows = lax.broadcasted_iota(jnp.int32, (tokens, q_ref.shape[2]), 0)

    def compute(work):
        done = []
        for slot, source, rank in work:
            block = source * per_pair + rank
            head = jnp.maximum(order_smem[source, 0, me * per_pair + rank], 0)
            done.append(item(
                recv[block, 0], recv[block, 1], recv[block, 2], state_ref[slot],
                table_ref[head_rate_ref[0, head]], length_ref[source], gaps, rows,
            ))
        for (slot, _, _), (result, final) in zip(work, done):
            rows_ref[slot] = result
            final_ref[slot] = final

    def arrived(block):
        pltpu.make_async_copy(recv.at[block], recv.at[block], recv_sem.at[block]).wait()

    loads[3].wait()
    order_copy.wait()
    if full:

        def own(rank, carry):
            compute([(me * per_pair + rank, me, rank)])
            return carry

        lax.fori_loop(0, per_pair, own, 0)

        def others(rank, carry):
            sources = [sender(step) for step in range(1, replicas)]
            for source in sources:
                arrived(source * per_pair + rank)
            compute([(source * per_pair + rank, source, rank) for source in sources])
            return carry

        lax.fori_loop(0, per_pair, others, 0)
    else:
        for rank in range(per_pair):
            for step in range(1, replicas):
                arrived(lax.rem(me + step, replicas) * per_pair + rank)

        def each(slot, carry):
            def scan(block, found):
                seen, chosen = found
                taken = order_smem[block // per_pair, 0, me * per_pair + block % per_pair] >= 0
                chosen = jnp.where(taken & (seen == slot), block, chosen)
                return seen + jnp.where(taken, 1, 0), chosen

            chosen = lax.fori_loop(
                0, replicas * per_pair, scan, (jnp.int32(0), jnp.int32(0))
            )[1]
            compute([(slot, chosen // per_pair, chosen % per_pair)])
            return carry

        lax.fori_loop(0, heads, each, 0)

    for rank in range(per_pair):
        for step in range(1, replicas):
            outgoing(step, rank).wait_send()


def local(queries, key_rows, value_rows, state_in, lengths, assignment, head_rate, decay_table):
    heads, tokens, size = queries.shape[2:]
    replicas = lax.axis_size("replica")
    per_pair = max(1, heads // replicas)
    slots = replicas * per_pair
    lanes = -(-slots // 128) * 128
    smem = pl.BlockSpec(memory_space=pltpu.SMEM)
    vmem = pl.BlockSpec(memory_space=pltpu.VMEM)
    held = pl.BlockSpec(memory_space=pltpu.HBM)
    block = pltpu.VMEM((heads, tokens, size), jnp.bfloat16)
    rows_out, final_out = pl.pallas_call(
        functools.partial(kernel, replicas, per_pair, slots == heads),
        out_shape=(
            pltpu.VMEM((heads, tokens, size), jnp.bfloat16),
            pltpu.VMEM((heads, size, size), jnp.float32),
        ),
        in_specs=[vmem] + [smem] * 3 + [held] * 4,
        out_specs=(vmem, vmem),
        scratch_shapes=[
            block, block, block,
            pltpu.VMEM((slots, 3, tokens, size), jnp.bfloat16),
            pltpu.VMEM((slots, 3, tokens, size), jnp.bfloat16),
            pltpu.VMEM((heads, size, size), jnp.float32),
            pltpu.VMEM((replicas, 1, lanes), jnp.int32),
            pltpu.SMEM((1, lanes), jnp.int32),
            pltpu.SMEM((replicas, 1, lanes), jnp.int32),
            pltpu.SemaphoreType.DMA((4,)),
            pltpu.SemaphoreType.DMA((2,)),
            pltpu.SemaphoreType.DMA((slots,)),
            pltpu.SemaphoreType.DMA((slots,)),
        ],
        compiler_params=pltpu.CompilerParams(
            collective_id=0, has_side_effects=True, vmem_limit_bytes=54 * 1024 * 1024
        ),
    )(
        assignment, lengths, head_rate, decay_table,
        queries[0, 0], key_rows[0, 0], value_rows[0, 0], state_in[0, 0],
    )
    return (rows_out[None, None], final_out[None, None])


def solution(mesh):
    in_specs = (
        P(("groups", "replica"), "section", "tensor", None, None),
        P(("groups", "replica"), "section", "tensor", None, None),
        P(("groups", "replica"), "section", "tensor", None, None),
        P(("groups", "replica"), "section", "tensor", None, None),
        P("groups"),
        P("groups", None, None),
        P("section", "tensor"),
        P(),
    )
    out_specs = (
        P(("groups", "replica"), "section", "tensor", None, None),
        P(("groups", "replica"), "section", "tensor", None, None),
    )
    return jax.shard_map(local, mesh=mesh, in_specs=in_specs, out_specs=out_specs, check_vma=False)
```

```python
import functools

import jax
import jax.numpy as jnp
from jax import lax
from jax.experimental import pallas as pl
from jax.experimental.pallas import tpu as pltpu
from jax.sharding import PartitionSpec as P

MESH = pl.DeviceIdType.MESH


def item(query, key, value, state, rate, count, gaps, rows):
    size = state.shape[1]
    scores = lax.dot_general(
        query, key, (((1,), (1,)), ((), ())), preferred_element_type=jnp.float32
    )
    weight = jnp.where(gaps >= 0.0, jnp.exp(-rate * jnp.maximum(gaps, 0.0)), 0.0)
    probs = (scores * weight).astype(jnp.bfloat16)
    intra = jnp.dot(probs, value, preferred_element_type=jnp.float32)
    high = state.astype(jnp.bfloat16)
    low = (state - high.astype(jnp.float32)).astype(jnp.bfloat16)
    mixed = jnp.dot(
        query, jnp.concatenate([high, low], axis=1), preferred_element_type=jnp.float32
    )
    mixed = mixed[:, :size] + mixed[:, size:]
    powers = jnp.exp(-rate * (rows.astype(jnp.float32) + 1.0))
    result = jnp.where(rows < count, intra + powers * mixed, 0.0).astype(jnp.bfloat16)
    remain = jnp.maximum(count - 1 - rows, 0).astype(jnp.float32)
    fade = jnp.where(rows < count, jnp.exp(-rate * remain), 0.0)
    scaled = value.astype(jnp.float32) * fade
    high = scaled.astype(jnp.bfloat16)
    low = (scaled - high.astype(jnp.float32)).astype(jnp.bfloat16)
    delta = lax.dot_general(
        key,
        jnp.concatenate([high, low], axis=1),
        (((0,), (0,)), ((), ())),
        preferred_element_type=jnp.float32,
    )
    delta = delta[:, :size] + delta[:, size:]
    kept = jnp.exp(jnp.full((1, size), -rate * count.astype(jnp.float32)))
    return result, kept * state + delta


def kernel(
    replicas, per_pair, full,
    asg_ref, length_ref, head_rate_ref, table_ref, q_hbm, k_hbm, v_hbm, state_hbm,
    rows_ref, final_ref,
    q_ref, k_ref, v_ref, send, recv, state_ref,
    order_vmem, own_smem, order_smem,
    load_sem, order_sem, send_sem, recv_sem,
):
    heads, tokens = q_ref.shape[0], q_ref.shape[1]
    me = lax.axis_index("replica")
    layer = lax.axis_index("section")
    first = lax.axis_index("tensor") * heads

    half = replicas // 2
    side, spot = me // half, me % half

    def receiver(step):
        if step <= half:
            return (1 - side) * half + (spot + step - 1) % half
        return side * half + (spot + step - half) % half

    def sender(step):
        if step <= half:
            return (1 - side) * half + (spot + half - (step - 1)) % half
        return side * half + (spot + half - (step - half)) % half

    barrier = pltpu.get_barrier_semaphore()
    for step in range(1, replicas):
        pl.semaphore_signal(
            barrier, inc=1, device_id={"replica": lax.rem(me + step, replicas)},
            device_id_type=MESH,
        )
    loads = [
        pltpu.make_async_copy(source, target, load_sem.at[number])
        for number, (source, target) in enumerate(
            ((q_hbm, q_ref), (k_hbm, k_ref), (v_hbm, v_ref), (state_hbm, state_ref))
        )
    ]
    for load in loads:
        load.start()

    width = asg_ref.shape[2]
    lanes = order_vmem.shape[2]
    layers = lax.broadcasted_iota(jnp.int32, (asg_ref.shape[1], width), 0)
    col = lax.broadcasted_iota(jnp.int32, (width, width), 1)
    row = lax.broadcasted_iota(jnp.int32, (width, width), 0)
    inside = (row >= first) & (row < first + heads)
    counted = (col >= first) & (col < row)
    pair = lax.broadcasted_iota(jnp.int32, (width, lanes), 1)
    head = lax.broadcasted_iota(jnp.int32, (width, lanes), 0) - first + 1

    def find(replica):
        named = jnp.sum(
            jnp.where(layers == layer, asg_ref[replica], 0), axis=0, keepdims=True
        )
        along = jnp.broadcast_to(named, (width, width))
        down = jnp.sum(jnp.where(row == col, along, 0), axis=1, keepdims=True)
        rank = jnp.sum(
            jnp.where(counted & (down == along), 1, 0), axis=1, keepdims=True
        )
        place = jnp.where(inside[:, :1], down * per_pair + rank, -1)
        order_vmem[replica] = (
            jnp.sum(jnp.where(place == pair, head, 0), axis=0, keepdims=True) - 1
        )

    find(me)
    own_copy = pltpu.make_async_copy(order_vmem.at[me], own_smem, order_sem.at[0])
    own_copy.start()
    for load in loads[:3]:
        load.wait()
    own_copy.wait()

    def stage(target, buffer, place):
        head = own_smem[0, target]
        if not full:
            head = jnp.maximum(head, 0)
        buffer[place, 0] = q_ref[head]
        buffer[place, 1] = k_ref[head]
        buffer[place, 2] = v_ref[head]

    chunk = 2 if per_pair % 2 == 0 else 1

    def outgoing(step, rank):
        return pltpu.make_async_remote_copy(
            src_ref=send.at[pl.ds(step * per_pair + rank, chunk)],
            dst_ref=recv.at[pl.ds(me * per_pair + rank, chunk)],
            send_sem=send_sem.at[step * per_pair + rank],
            recv_sem=recv_sem.at[me * per_pair + rank],
            device_id={"replica": receiver(step)},
            device_id_type=MESH,
        )

    for rank in range(0, per_pair, chunk):
        for step in range(1, replicas):
            target = receiver(step)
            for one in range(rank, rank + chunk):
                stage(target * per_pair + one, send, step * per_pair + one)
            if rank == 0 and step == 1:
                pl.semaphore_wait(barrier, replicas - 1)
            outgoing(step, rank).start()

    def find_other(step, carry):
        find(lax.rem(me + step, replicas))
        return carry

    lax.fori_loop(1, replicas, find_other, 0)
    order_copy = pltpu.make_async_copy(order_vmem, order_smem, order_sem.at[1])
    order_copy.start()

    def stage_own(rank, carry):
        stage(me * per_pair + rank, recv, me * per_pair + rank)
        return carry

    lax.fori_loop(0, per_pair, stage_own, 0)

    across = lax.broadcasted_iota(jnp.int32, (tokens, tokens), 1)
    down = lax.broadcasted_iota(jnp.int32, (tokens, tokens), 0)
    gaps = (down - across).astype(jnp.float32)
    rows = lax.broadcasted_iota(jnp.int32, (tokens, q_ref.shape[2]), 0)

    def compute(work):
        done = []
        for slot, source, rank in work:
            block = source * per_pair + rank
            head = jnp.maximum(order_smem[source, 0, me * per_pair + rank], 0)
            done.append(item(
                recv[block, 0], recv[block, 1], recv[block, 2], state_ref[slot],
                table_ref[head_rate_ref[0, head]], length_ref[source], gaps, rows,
            ))
        for (slot, _, _), (result, final) in zip(work, done):
            rows_ref[slot] = result
            final_ref[slot] = final

    def arrived(block):
        held = recv.at[pl.ds(block, chunk)]
        pltpu.make_async_copy(held, held, recv_sem.at[block]).wait()

    loads[3].wait()
    order_copy.wait()
    if full:

        def own(rank, carry):
            compute([(me * per_pair + rank, me, rank)])
            return carry

        lax.fori_loop(0, per_pair, own, 0)

        def others(turn, carry):
            sources = [sender(step) for step in range(1, replicas)]
            for source in sources:
                arrived(source * per_pair + turn * chunk)
            for one in range(chunk):
                rank = turn * chunk + one
                compute([(source * per_pair + rank, source, rank) for source in sources])
            return carry

        lax.fori_loop(0, per_pair // chunk, others, 0)
    else:
        for rank in range(0, per_pair, chunk):
            for step in range(1, replicas):
                arrived(lax.rem(me + step, replicas) * per_pair + rank)

        def each(slot, carry):
            def scan(block, found):
                seen, chosen = found
                taken = order_smem[block // per_pair, 0, me * per_pair + block % per_pair] >= 0
                chosen = jnp.where(taken & (seen == slot), block, chosen)
                return seen + jnp.where(taken, 1, 0), chosen

            chosen = lax.fori_loop(
                0, replicas * per_pair, scan, (jnp.int32(0), jnp.int32(0))
            )[1]
            compute([(slot, chosen // per_pair, chosen % per_pair)])
            return carry

        lax.fori_loop(0, heads, each, 0)

    for rank in range(0, per_pair, chunk):
        for step in range(1, replicas):
            outgoing(step, rank).wait_send()


def local(queries, key_rows, value_rows, state_in, lengths, assignment, head_rate, decay_table):
    heads, tokens, size = queries.shape[2:]
    replicas = lax.axis_size("replica")
    per_pair = max(1, heads // replicas)
    slots = replicas * per_pair
    lanes = -(-slots // 128) * 128
    smem = pl.BlockSpec(memory_space=pltpu.SMEM)
    vmem = pl.BlockSpec(memory_space=pltpu.VMEM)
    held = pl.BlockSpec(memory_space=pltpu.HBM)
    block = pltpu.VMEM((heads, tokens, size), jnp.bfloat16)
    rows_out, final_out = pl.pallas_call(
        functools.partial(kernel, replicas, per_pair, slots == heads),
        out_shape=(
            pltpu.VMEM((heads, tokens, size), jnp.bfloat16),
            pltpu.VMEM((heads, size, size), jnp.float32),
        ),
        in_specs=[vmem] + [smem] * 3 + [held] * 4,
        out_specs=(vmem, vmem),
        scratch_shapes=[
            block, block, block,
            pltpu.VMEM((slots, 3, tokens, size), jnp.bfloat16),
            pltpu.VMEM((slots, 3, tokens, size), jnp.bfloat16),
            pltpu.VMEM((heads, size, size), jnp.float32),
            pltpu.VMEM((replicas, 1, lanes), jnp.int32),
            pltpu.SMEM((1, lanes), jnp.int32),
            pltpu.SMEM((replicas, 1, lanes), jnp.int32),
            pltpu.SemaphoreType.DMA((4,)),
            pltpu.SemaphoreType.DMA((2,)),
            pltpu.SemaphoreType.DMA((slots,)),
            pltpu.SemaphoreType.DMA((slots,)),
        ],
        compiler_params=pltpu.CompilerParams(
            collective_id=0, has_side_effects=True, vmem_limit_bytes=54 * 1024 * 1024
        ),
    )(
        assignment, lengths, head_rate, decay_table,
        queries[0, 0], key_rows[0, 0], value_rows[0, 0], state_in[0, 0],
    )
    return (rows_out[None, None], final_out[None, None])


def solution(mesh):
    in_specs = (
        P(("groups", "replica"), "section", "tensor", None, None),
        P(("groups", "replica"), "section", "tensor", None, None),
        P(("groups", "replica"), "section", "tensor", None, None),
        P(("groups", "replica"), "section", "tensor", None, None),
        P("groups"),
        P("groups", None, None),
        P("section", "tensor"),
        P(),
    )
    out_specs = (
        P(("groups", "replica"), "section", "tensor", None, None),
        P(("groups", "replica"), "section", "tensor", None, None),
    )
    return jax.shard_map(local, mesh=mesh, in_specs=in_specs, out_specs=out_specs, check_vma=False)
```

```python
import functools

import jax
import jax.numpy as jnp
from jax import lax
from jax.experimental import pallas as pl
from jax.experimental.pallas import tpu as pltpu
from jax.sharding import PartitionSpec as P

MESH = pl.DeviceIdType.MESH


def item(query, key, value, state, rate, count, gaps, rows):
    size = state.shape[1]
    scores = lax.dot_general(
        query, key, (((1,), (1,)), ((), ())), preferred_element_type=jnp.float32
    )
    weight = jnp.where(gaps >= 0.0, jnp.exp(-rate * jnp.maximum(gaps, 0.0)), 0.0)
    probs = (scores * weight).astype(jnp.bfloat16)
    intra = jnp.dot(probs, value, preferred_element_type=jnp.float32)
    high = state.astype(jnp.bfloat16)
    low = (state - high.astype(jnp.float32)).astype(jnp.bfloat16)
    mixed = jnp.dot(
        query, jnp.concatenate([high, low], axis=1), preferred_element_type=jnp.float32
    )
    mixed = mixed[:, :size] + mixed[:, size:]
    powers = jnp.exp(-rate * (rows.astype(jnp.float32) + 1.0))
    result = jnp.where(rows < count, intra + powers * mixed, 0.0).astype(jnp.bfloat16)
    remain = jnp.maximum(count - 1 - rows, 0).astype(jnp.float32)
    fade = jnp.where(rows < count, jnp.exp(-rate * remain), 0.0)
    scaled = value.astype(jnp.float32) * fade
    high = scaled.astype(jnp.bfloat16)
    low = (scaled - high.astype(jnp.float32)).astype(jnp.bfloat16)
    delta = lax.dot_general(
        key,
        jnp.concatenate([high, low], axis=1),
        (((0,), (0,)), ((), ())),
        preferred_element_type=jnp.float32,
    )
    delta = delta[:, :size] + delta[:, size:]
    kept = jnp.exp(jnp.full((1, size), -rate * count.astype(jnp.float32)))
    return result, kept * state + delta


def kernel(
    replicas, per_pair, full,
    asg_ref, length_ref, head_rate_ref, table_ref, q_hbm, k_hbm, v_hbm, state_hbm,
    rows_ref, final_ref,
    q_ref, k_ref, v_ref, send, recv, state_ref,
    order_vmem, own_smem, order_smem,
    load_sem, order_sem, send_sem, recv_sem,
):
    heads, tokens = q_ref.shape[0], q_ref.shape[1]
    me = lax.axis_index("replica")
    layer = lax.axis_index("section")
    first = lax.axis_index("tensor") * heads

    half = replicas // 2
    side, spot = me // half, me % half

    def receiver(step):
        if step <= half:
            return (1 - side) * half + (spot + step - 1) % half
        return side * half + (spot + step - half) % half

    def sender(step):
        if step <= half:
            return (1 - side) * half + (spot + half - (step - 1)) % half
        return side * half + (spot + half - (step - half)) % half

    barrier = pltpu.get_barrier_semaphore()
    for step in range(1, replicas):
        pl.semaphore_signal(
            barrier, inc=1, device_id={"replica": lax.rem(me + step, replicas)},
            device_id_type=MESH,
        )
    loads = [
        pltpu.make_async_copy(source, target, load_sem.at[number])
        for number, (source, target) in enumerate(
            ((q_hbm, q_ref), (k_hbm, k_ref), (v_hbm, v_ref), (state_hbm, state_ref))
        )
    ]
    for load in loads[:3]:
        load.start()

    width = asg_ref.shape[2]
    lanes = order_vmem.shape[2]
    layers = lax.broadcasted_iota(jnp.int32, (asg_ref.shape[1], width), 0)
    col = lax.broadcasted_iota(jnp.int32, (width, width), 1)
    row = lax.broadcasted_iota(jnp.int32, (width, width), 0)
    inside = (row >= first) & (row < first + heads)
    counted = (col >= first) & (col < row)
    pair = lax.broadcasted_iota(jnp.int32, (width, lanes), 1)
    head = lax.broadcasted_iota(jnp.int32, (width, lanes), 0) - first + 1

    def find(replica):
        named = jnp.sum(
            jnp.where(layers == layer, asg_ref[replica], 0), axis=0, keepdims=True
        )
        along = jnp.broadcast_to(named, (width, width))
        down = jnp.sum(jnp.where(row == col, along, 0), axis=1, keepdims=True)
        rank = jnp.sum(
            jnp.where(counted & (down == along), 1, 0), axis=1, keepdims=True
        )
        place = jnp.where(inside[:, :1], down * per_pair + rank, -1)
        order_vmem[replica] = (
            jnp.sum(jnp.where(place == pair, head, 0), axis=0, keepdims=True) - 1
        )

    find(me)
    own_copy = pltpu.make_async_copy(order_vmem.at[me], own_smem, order_sem.at[0])
    own_copy.start()
    for load in loads[:3]:
        load.wait()
    own_copy.wait()

    def stage(target, buffer, place):
        head = own_smem[0, target]
        if not full:
            head = jnp.maximum(head, 0)
        buffer[place, 0] = q_ref[head]
        buffer[place, 1] = k_ref[head]
        buffer[place, 2] = v_ref[head]

    chunk = 2 if per_pair % 2 == 0 else 1

    def outgoing(step, rank):
        return pltpu.make_async_remote_copy(
            src_ref=send.at[pl.ds(step * per_pair + rank, chunk)],
            dst_ref=recv.at[pl.ds(me * per_pair + rank, chunk)],
            send_sem=send_sem.at[step * per_pair + rank],
            recv_sem=recv_sem.at[me * per_pair + rank],
            device_id={"replica": receiver(step)},
            device_id_type=MESH,
        )

    for rank in range(0, per_pair, chunk):
        for step in range(1, replicas):
            target = receiver(step)
            for one in range(rank, rank + chunk):
                stage(target * per_pair + one, send, step * per_pair + one)
            if rank == 0 and step == 1:
                pl.semaphore_wait(barrier, replicas - 1)
            outgoing(step, rank).start()

    loads[3].start()

    def find_other(step, carry):
        find(lax.rem(me + step, replicas))
        return carry

    lax.fori_loop(1, replicas, find_other, 0)
    order_copy = pltpu.make_async_copy(order_vmem, order_smem, order_sem.at[1])
    order_copy.start()

    def stage_own(rank, carry):
        stage(me * per_pair + rank, recv, me * per_pair + rank)
        return carry

    lax.fori_loop(0, per_pair, stage_own, 0)

    across = lax.broadcasted_iota(jnp.int32, (tokens, tokens), 1)
    down = lax.broadcasted_iota(jnp.int32, (tokens, tokens), 0)
    gaps = (down - across).astype(jnp.float32)
    rows = lax.broadcasted_iota(jnp.int32, (tokens, q_ref.shape[2]), 0)

    def compute(work):
        done = []
        for slot, source, rank in work:
            block = source * per_pair + rank
            head = jnp.maximum(order_smem[source, 0, me * per_pair + rank], 0)
            done.append(item(
                recv[block, 0], recv[block, 1], recv[block, 2], state_ref[slot],
                table_ref[head_rate_ref[0, head]], length_ref[source], gaps, rows,
            ))
        for (slot, _, _), (result, final) in zip(work, done):
            rows_ref[slot] = result
            final_ref[slot] = final

    def arrived(block):
        held = recv.at[pl.ds(block, chunk)]
        pltpu.make_async_copy(held, held, recv_sem.at[block]).wait()

    loads[3].wait()
    order_copy.wait()
    if full:

        def own(rank, carry):
            compute([(me * per_pair + rank, me, rank)])
            return carry

        lax.fori_loop(0, per_pair, own, 0)

        def others(turn, carry):
            sources = [sender(step) for step in range(1, replicas)]
            for source in sources:
                arrived(source * per_pair + turn * chunk)
            for one in range(chunk):
                rank = turn * chunk + one
                compute([(source * per_pair + rank, source, rank) for source in sources])
            return carry

        lax.fori_loop(0, per_pair // chunk, others, 0)
    else:
        for rank in range(0, per_pair, chunk):
            for step in range(1, replicas):
                arrived(lax.rem(me + step, replicas) * per_pair + rank)

        def each(slot, carry):
            def scan(block, found):
                seen, chosen = found
                taken = order_smem[block // per_pair, 0, me * per_pair + block % per_pair] >= 0
                chosen = jnp.where(taken & (seen == slot), block, chosen)
                return seen + jnp.where(taken, 1, 0), chosen

            chosen = lax.fori_loop(
                0, replicas * per_pair, scan, (jnp.int32(0), jnp.int32(0))
            )[1]
            compute([(slot, chosen // per_pair, chosen % per_pair)])
            return carry

        lax.fori_loop(0, heads, each, 0)

    for rank in range(0, per_pair, chunk):
        for step in range(1, replicas):
            outgoing(step, rank).wait_send()


def local(queries, key_rows, value_rows, state_in, lengths, assignment, head_rate, decay_table):
    heads, tokens, size = queries.shape[2:]
    replicas = lax.axis_size("replica")
    per_pair = max(1, heads // replicas)
    slots = replicas * per_pair
    lanes = -(-slots // 128) * 128
    smem = pl.BlockSpec(memory_space=pltpu.SMEM)
    vmem = pl.BlockSpec(memory_space=pltpu.VMEM)
    held = pl.BlockSpec(memory_space=pltpu.HBM)
    block = pltpu.VMEM((heads, tokens, size), jnp.bfloat16)
    rows_out, final_out = pl.pallas_call(
        functools.partial(kernel, replicas, per_pair, slots == heads),
        out_shape=(
            pltpu.VMEM((heads, tokens, size), jnp.bfloat16),
            pltpu.VMEM((heads, size, size), jnp.float32),
        ),
        in_specs=[vmem] + [smem] * 3 + [held] * 4,
        out_specs=(vmem, vmem),
        scratch_shapes=[
            block, block, block,
            pltpu.VMEM((slots, 3, tokens, size), jnp.bfloat16),
            pltpu.VMEM((slots, 3, tokens, size), jnp.bfloat16),
            pltpu.VMEM((heads, size, size), jnp.float32),
            pltpu.VMEM((replicas, 1, lanes), jnp.int32),
            pltpu.SMEM((1, lanes), jnp.int32),
            pltpu.SMEM((replicas, 1, lanes), jnp.int32),
            pltpu.SemaphoreType.DMA((4,)),
            pltpu.SemaphoreType.DMA((2,)),
            pltpu.SemaphoreType.DMA((slots,)),
            pltpu.SemaphoreType.DMA((slots,)),
        ],
        compiler_params=pltpu.CompilerParams(
            collective_id=0, has_side_effects=True, vmem_limit_bytes=54 * 1024 * 1024
        ),
    )(
        assignment, lengths, head_rate, decay_table,
        queries[0, 0], key_rows[0, 0], value_rows[0, 0], state_in[0, 0],
    )
    return (rows_out[None, None], final_out[None, None])


def solution(mesh):
    in_specs = (
        P(("groups", "replica"), "section", "tensor", None, None),
        P(("groups", "replica"), "section", "tensor", None, None),
        P(("groups", "replica"), "section", "tensor", None, None),
        P(("groups", "replica"), "section", "tensor", None, None),
        P("groups"),
        P("groups", None, None),
        P("section", "tensor"),
        P(),
    )
    out_specs = (
        P(("groups", "replica"), "section", "tensor", None, None),
        P(("groups", "replica"), "section", "tensor", None, None),
    )
    return jax.shard_map(local, mesh=mesh, in_specs=in_specs, out_specs=out_specs, check_vma=False)
```
